768 devices in a mesh: path: 12 (over x, z_hi), fsdp: 64 (over y, z_lo, core).
Axes of the slice: x: 4, y: 8, z: 12 (z_hi: 3, z_lo: 4; z = z_hi * 4 + z_lo), core: 2. Of those that a mesh axis runs over, the one named last changes fastest.
Arguments:
- tokens: bfloat16 [12, 1024, 4096], P('path', 'fsdp'), may hold values from -6 to 6
- up_values: bfloat16 [12, 1024, 7680], P('path', None, 'fsdp'), may hold values from -6 to 6
- out_grad: bfloat16 [12, 1024, 7680], P('path', None, 'fsdp'), may hold values from -6 to 6
- weights: bfloat16 [12, 4096, 7680], P('path', None, 'fsdp'), may hold values from -6 to 6
- momentum: float32 [12, 4096, 7680], P('path', None, 'fsdp'), may hold values from -1.5 to 1.5
- path_table: int32 [12, 1], replicated, may hold values from 0 to 15, as said below
- live_tokens: int32 [12], P('path'), may hold values from 256 to 1024, as said below
Outputs:
- new_weights: bfloat16 [12, 4096, 7680], P('path', None, 'fsdp')
The draws below stay inside these ranges and needn't reach their ends.
Inputs may be any that keep to these rules, and one draw needn't show every extreme that they name: `path_table`: module ids of the level; several groups share some modules, others hold a module alone. Routed tokens fill positions 0 to live_tokens[g] - 1 of a group's block.
All inputs are finite; a program needn't handle non-finite values.
Results may differ from the reference program's by a relative error of at most 0.0034.
Values may be sent and summed in bfloat16 or wider, within the bound.
A program may use at most 64 MiB of HBM per device.

```python
import jax
import jax.numpy as jnp
from jax import lax

D = 4096
FF = 7680
MODULES = 16
TOK = 1024
N_PATH = 12


def draw_path_table(key, part):
    key = jax.random.fold_in(key, 11)
    first, second, third = jax.random.split(key, 3)
    pool = 1 + jax.random.permutation(third, MODULES - 2)
    picks = jax.random.randint(first, (N_PATH,), 0, max(2, N_PATH // 3))
    base = pool[picks]
    order = jax.random.permutation(second, N_PATH)
    base = base.at[order[3]].set(base[order[2]])
    base = base.at[order[0]].set(0).at[order[1]].set(MODULES - 1)
    return base[:, None].astype(jnp.int32)


def draw_live_tokens(key, part):
    key = jax.random.fold_in(key, 23)
    first, second = jax.random.split(key)
    counts = jax.random.randint(first, (N_PATH,), TOK // 4, TOK + 1)
    order = jax.random.permutation(second, N_PATH)
    counts = counts.at[order[0]].set(TOK).at[order[1]].set(TOK // 4)
    return counts.astype(jnp.int32)


def level_of(key, dims, cuts, smallest, high):
    gain, own = 1.0, jax.random.fold_in(key, 6)
    for dim, parts in cuts:
        steps = jnp.exp(jax.random.uniform(jax.random.fold_in(own, dim), (parts,), jnp.float32, smallest / len(cuts), high / len(cuts)))
        gain = gain * jnp.repeat(steps, dims[dim] // parts).reshape([-1 if axis == dim else 1 for axis in range(len(dims))])
    return gain


def normal_values(stream_key, extent, spread, bound, cuts=(), held_as=jnp.bfloat16):
    array = jax.random.normal(stream_key, extent, jnp.float32) * spread
    if len(cuts) > 0:
        array = level_of(stream_key, extent, cuts, -0.22, 0.18) * array
    return jnp.clip(array, min=-bound, max=bound).astype(held_as)


def setup_inputs(seed: int = 0) -> dict:
    arg_keys = jax.random.split(jax.random.key(seed), 8)
    tokens = normal_values(arg_keys[0], (N_PATH, TOK, D), 1.0, 6.0, ((0, 12), (1, 64)))
    up_values = normal_values(arg_keys[1], (N_PATH, TOK, FF), 1.0, 6.0, ((0, 12), (2, 64)))
    out_grad = normal_values(arg_keys[2], (N_PATH, TOK, FF), 1.0, 6.0, ((0, 12), (2, 64)))
    weights = normal_values(arg_keys[3], (N_PATH, D, FF), 1.0, 6.0, ((0, 12), (2, 64)))
    momentum = normal_values(arg_keys[4], (N_PATH, D, FF), 0.25, 1.5, ((0, 12), (2, 64)), jnp.float32)
    path_table = draw_path_table(jax.random.fold_in(arg_keys[7], 71), 0)
    live_tokens = draw_live_tokens(jax.random.fold_in(arg_keys[7], 71), 0)
    return dict(tokens=tokens, up_values=up_values, out_grad=out_grad, weights=weights, momentum=momentum, path_table=path_table, live_tokens=live_tokens)


def group_grad(args):
    tokens, up_values, out_grad, weights, live = args
    scale = 1.0 / D ** 0.5
    gate = jnp.dot(tokens, weights, preferred_element_type=jnp.float32) * scale
    sig = jax.nn.sigmoid(gate)
    slope = sig * (1.0 + gate * (1.0 - sig))
    keep = jnp.arange(TOK, dtype=jnp.int32) < live
    term = out_grad.astype(jnp.float32) * up_values.astype(jnp.float32) * slope
    gate_grad = jnp.where(keep[:, None], term, 0.0).astype(jnp.bfloat16)
    total = jnp.dot(tokens.T, gate_grad, preferred_element_type=jnp.float32)
    return (total * scale).astype(jnp.bfloat16)

def reference(tokens, up_values, out_grad, weights, momentum, path_table, live_tokens):
    pseudo = lax.map(group_grad, (tokens, up_values, out_grad, weights, live_tokens))
    ids = path_table[:, 0]
    share = (ids[:, None] == ids[None, :]).astype(jnp.float32)
    count = lax.optimization_barrier(jnp.sum(share, axis=1))

    def update(args):
        share_row, count_one, weight_one, moment_one = args

        def add_group(index, acc):
            return acc + share_row[index] * pseudo[index].astype(jnp.float32)
        acc = lax.fori_loop(0, N_PATH, add_group, jnp.zeros((D, FF), jnp.float32))
        averaged = (acc / count_one).astype(jnp.bfloat16).astype(jnp.float32)
        new_moment = 0.9 * moment_one + averaged
        fresh = weight_one.astype(jnp.float32) - 0.7 * (averaged + 0.9 * new_moment)
        return fresh.astype(jnp.bfloat16)
    return lax.map(update, (share, count, weights, momentum))
```

```python
import jax
import jax.numpy as jnp
from jax import lax
from jax.experimental import pallas as pl
from jax.experimental.pallas import tpu as pltpu
from jax.sharding import PartitionSpec as P

MESH = pl.DeviceIdType.MESH

NX, ZH, NY, ZL = 4, 3, 8, 4
NP = NX * ZH
D, TOK, COLS = 4096, 1024, 120
ROWS = TOK // (NY * ZL * 2)
BUNDLE = ROWS * ZL * 2
QUARTER = D // NX
THIRD = COLS // ZH
CHUNKS = 2
LANES = 256
PART = THIRD * QUARTER // (CHUNKS * LANES)
SUBS = PART // THIRD

SLOT = {0: 0, 4: 1, 1: 2, -1: 3, 2: 4, -2: 5, 3: 6, -3: 7}


def body(
    tok_in, up_in, og_in, w_in, mom_in, table, live, out,
    tok, up, og, w, mom, acc, psend, precv, asend, arecv, fresh, share, inv,
    load_sem, own_sem, z_send, z_recv, y_send, y_recv, c_send, c_recv,
    p_send, p_recv, a_send, a_recv, out_sem,
):
    path = lax.axis_index("path")
    fsdp = lax.axis_index("fsdp")
    core = fsdp % 2
    z = (fsdp // 2) % ZL
    y = fsdp // (2 * ZL)
    x = path // ZH
    third = path % ZH

    def at(yy, zz, cc):
        return (path, (yy * ZL + zz) * 2 + cc)

    order = (z, z + 1 - 2 * (z % 2), 2 - z // 2, 3 - 3 * (z // 2))
    up_y, down_y = at((y + 1) % NY, z, core), at((y + NY - 1) % NY, z, core)
    sibling = at(y, z, 1 - core)

    loads = [
        pltpu.make_async_copy(src, dst, load_sem.at[i])
        for i, (src, dst) in enumerate(((w_in, w), (up_in, up), (og_in, og), (mom_in, mom)))
    ]

    def rows(rel, k):
        return pl.ds(pl.multiple_of(SLOT[rel] * BUNDLE + (order[k] * 2 + core) * ROWS, ROWS), ROWS)

    own = pltpu.make_async_copy(tok_in, tok.at[rows(0, 0)], own_sem)
    own.start()
    for load in loads:
        load.start()

    barrier = pltpu.get_barrier_semaphore()
    friends = [up_y, down_y, sibling]
    friends += [at(y, order[k], core) for k in range(1, ZL)]
    friends += [((path + o) % NP, fsdp) for o in range(1, NP)]
    for friend in friends:
        pl.semaphore_signal(barrier, inc=1, device_id=friend, device_id_type=MESH)
    pl.semaphore_wait(barrier, len(friends))

    def z_copy(k):
        return pltpu.make_async_remote_copy(
            src_ref=tok_in, dst_ref=tok.at[rows(0, 0)], send_sem=z_send.at[k], recv_sem=z_recv.at[z],
            device_id=at(y, order[k], core), device_id_type=MESH,
        )

    def z_arrival(k):
        return pltpu.make_async_remote_copy(
            src_ref=tok_in, dst_ref=tok.at[rows(0, k)], send_sem=z_send.at[k], recv_sem=z_recv.at[order[k]],
            device_id=at(y, order[k], core), device_id_type=MESH,
        )

    def y_copy(way, step, k):
        sign = (-1, 1)[way]
        before, after = sign * (step - 1), sign * step
        after = 4 if after == -4 else after
        src = tok_in if step == 1 and k == 0 else tok.at[rows(before, k)]
        return pltpu.make_async_remote_copy(
            src_ref=src, dst_ref=tok.at[rows(after, k)],
            send_sem=y_send.at[way, step - 1, k], recv_sem=y_recv.at[way, step - 1, k],
            device_id=(up_y, down_y)[way], device_id_type=MESH,
        )

    def c_copy(rel, k):
        src = tok_in if rel == 0 and k == 0 else tok.at[rows(rel, k)]
        return pltpu.make_async_remote_copy(
            src_ref=src, dst_ref=tok.at[rows(rel, k)],
            send_sem=c_send.at[SLOT[rel], k], recv_sem=c_recv.at[SLOT[rel], k],
            device_id=sibling, device_id_type=MESH,
        )

    def sent(way, step, k):
        return step < 4 or (k < 2) == (way == 0)

    def gate_and_grad(rels, first):
        start, count = SLOT[rels[0]] * BUNDLE, len(rels) * BUNDLE
        gate = lax.dot_general(
            w[...], tok[start : start + count], (((1,), (1,)), ((), ())), preferred_element_type=jnp.float32
        ) * (1.0 / D**0.5)
        parts = []
        for i, rel in enumerate(rels):
            here = (y + rel + NY) % NY * BUNDLE
            lanes = pl.ds(pl.multiple_of(here, BUNDLE), BUNDLE)
            g = gate[:, i * BUNDLE : (i + 1) * BUNDLE]
            sig = jax.nn.sigmoid(g)
            slope = sig * (1.0 + g * (1.0 - sig))
            term = og[:, lanes].astype(jnp.float32) * up[:, lanes].astype(jnp.float32) * slope
            token = here + lax.broadcasted_iota(jnp.int32, (COLS, BUNDLE), 1)
            parts.append(jnp.where(token < live[0], term, 0.0).astype(jnp.bfloat16))
        return start, count, parts[0] if len(parts) == 1 else jnp.concatenate(parts, axis=1)

    def accumulate(rels, first):
        start, count, grad = gate_and_grad(rels, first)
        for q in range(NX):
            lanes = slice(q * QUARTER, (q + 1) * QUARTER)
            term = jnp.dot(grad, tok[start : start + count, lanes], preferred_element_type=jnp.float32)
            if first:
                acc[:, lanes] = term
            else:
                acc[:, lanes] += term

    def wait_sibling(rel):
        for k in range(ZL):
            c_copy(rel, k).wait_recv()

    for k in range(1, ZL):
        z_copy(k).start()
    for way in (0, 1):
        y_copy(way, 1, 0).start()
    c_copy(0, 0).start()
    for g in range(NP):
        total = jnp.float32(0.0)
        for h in range(NP):
            same = jnp.where(table[g] == table[h], 1.0, 0.0).astype(jnp.float32)
            share[g * NP + h] = same
            total = total + same
        inv[g] = 1.0 / total
    own.wait()
    for k in range(1, ZL):
        z_arrival(k).wait_recv()
        for way in (0, 1):
            y_copy(way, 1, k).start()
        c_copy(0, k).start()
    for load in loads[:3]:
        load.wait()

    def ring(step):
        for k in range(ZL):
            for way in (0, 1):
                if sent(way, step, k):
                    y_copy(way, step, k).wait_recv()
                    if step < 4 and sent(way, step + 1, k):
                        y_copy(way, step + 1, k).start()
                    c_copy((-1, 1)[way] * step if step < 4 else 4, k).start()

    wait_sibling(0)
    accumulate((0,), True)
    for step in (1, 2, 3):
        ring(step)
        if step > 1:
            wait_sibling(step - 1)
            wait_sibling(1 - step)
            accumulate((step - 1, 1 - step), False)
    wait_sibling(3)
    wait_sibling(-3)
    accumulate((3, -3), False)
    ring(4)
    wait_sibling(4)

    def p_copy(chunk, dest):
        return pltpu.make_async_remote_copy(
            src_ref=psend.at[chunk, dest], dst_ref=precv.at[chunk, path],
            send_sem=p_send.at[chunk, dest], recv_sem=p_recv.at[chunk, path],
            device_id=(dest, fsdp), device_id_type=MESH,
        )

    def p_arrival(chunk, source):
        return pltpu.make_async_remote_copy(
            src_ref=psend.at[chunk, source], dst_ref=precv.at[chunk, source],
            send_sem=p_send.at[chunk, source], recv_sem=p_recv.at[chunk, source],
            device_id=(source, fsdp), device_id_type=MESH,
        )

    def a_copy(chunk, dest):
        return pltpu.make_async_remote_copy(
            src_ref=asend.at[chunk, dest], dst_ref=arecv.at[chunk, path],
            send_sem=a_send.at[chunk, dest], recv_sem=a_recv.at[chunk, path],
            device_id=(dest, fsdp), device_id_type=MESH,
        )

    def a_arrival(chunk, source):
        return pltpu.make_async_remote_copy(
            src_ref=asend.at[chunk, source], dst_ref=arecv.at[chunk, source],
            send_sem=a_send.at[chunk, source], recv_sem=a_recv.at[chunk, source],
            device_id=(source, fsdp), device_id_type=MESH,
        )

    start, count, grad = gate_and_grad((4,), False)
    for j in range(NX):
        q = (x + j) % NX
        lanes = pl.ds(pl.multiple_of(q * QUARTER, QUARTER), QUARTER)
        total = acc[:, lanes] + jnp.dot(grad, tok[start : start + count, lanes], preferred_element_type=jnp.float32)
        total = total * (1.0 / D**0.5)
        for chunk in range(CHUNKS):
            for i in range(ZH):
                r = (third + 1 + i) % ZH
                dest = q * ZH + r
                first = chunk * SUBS * LANES
                for rr in range(ZH):
                    piece = jnp.concatenate(
                        [
                            total[rr * THIRD : (rr + 1) * THIRD, first + s * LANES : first + (s + 1) * LANES]
                            for s in range(SUBS)
                        ],
                        axis=0,
                    ).astype(jnp.bfloat16)
                    if i == 0:
                        psend[chunk, q * ZH + rr] = piece
                if j > 0 or i < ZH - 1:
                    p_copy(chunk, dest).start()

    for chunk in range(CHUNKS):
        for o in range(1, NP):
            p_arrival(chunk, (path + o) % NP).wait_recv()
        mine = pltpu.make_async_copy(psend.at[chunk, path], precv.at[chunk, path], own_sem)
        mine.start()
        mine.wait()

        @pl.loop(0, PART // 16)
        def _(i):
            part = pl.ds(pl.multiple_of(i * 16, 16), 16)
            values = [precv[chunk, h, part].astype(jnp.float32) for h in range(NP)]
            for g in range(NP):
                total = share[g * NP] * values[0]
                for h in range(1, NP):
                    total = total + share[g * NP + h] * values[h]
                asend[chunk, g, part] = (total * inv[g]).astype(jnp.bfloat16)

        for o in range(1, NP):
            a_copy(chunk, (path + o) % NP).start()

    loads[3].wait()
    writes = []
    for chunk in range(CHUNKS):
        mine = pltpu.make_async_copy(asend.at[chunk, path], arecv.at[chunk, path], own_sem)
        mine.start()
        mine.wait()
        for o in range(1, NP):
            a_arrival(chunk, (path + o) % NP).wait_recv()
        for q in range(NX):
            for s in range(SUBS):
                lanes = slice(q * QUARTER + (chunk * SUBS + s) * LANES, q * QUARTER + (chunk * SUBS + s + 1) * LANES)
                averaged = jnp.concatenate(
                    [
                        arecv[chunk, q * ZH + r].astype(jnp.float32)[s * THIRD : (s + 1) * THIRD]
                        for r in range(ZH)
                    ],
                    axis=0,
                )
                moment = 0.9 * mom[:, lanes] + averaged
                new = w[:, lanes].astype(jnp.float32) - 0.7 * (averaged + 0.9 * moment)
                fresh[:, lanes] = new.astype(jnp.bfloat16)
    write = pltpu.make_async_copy(fresh, out, out_sem)
    write.start()

    for k in range(1, ZL):
        z_copy(k).wait_send()
    for step in range(1, 5):
        for k in range(ZL):
            for way in (0, 1):
                if sent(way, step, k):
                    y_copy(way, step, k).wait_send()
    for rel in SLOT:
        for k in range(ZL):
            c_copy(rel, k).wait_send()
    for chunk in range(CHUNKS):
        for o in range(1, NP):
            p_copy(chunk, (path + o) % NP).wait_send()
            a_copy(chunk, (path + o) % NP).wait_send()
    write.wait()


def on_device(tokens, up_values, out_grad, weights, momentum, path_table, live_tokens):
    dma = pltpu.SemaphoreType.DMA
    bf16, f32 = jnp.bfloat16, jnp.float32
    anywhere = pl.BlockSpec(memory_space=pl.ANY)
    scalars = pl.BlockSpec(memory_space=pltpu.SMEM)
    shard = pltpu.VMEM((CHUNKS, NP, PART, LANES), bf16)
    new = pl.pallas_call(
        body,
        out_shape=jax.ShapeDtypeStruct((COLS, D), bf16),
        in_specs=[anywhere] * 5 + [scalars] * 2,
        out_specs=anywhere,
        scratch_shapes=[
            pltpu.VMEM((TOK, D), bf16),
            pltpu.VMEM((COLS, TOK), bf16),
            pltpu.VMEM((COLS, TOK), bf16),
            pltpu.VMEM((COLS, D), bf16),
            pltpu.VMEM((COLS, D), f32),
            pltpu.VMEM((COLS, D), f32),
            shard, shard, shard, shard,
            pltpu.VMEM((COLS, D), bf16),
            pltpu.SMEM((NP * NP,), f32),
            pltpu.SMEM((NP,), f32),
            dma((4,)),
            dma,
            dma((ZL,)), dma((ZL,)),
            dma((2, 4, ZL)), dma((2, 4, ZL)),
            dma((NY, ZL)), dma((NY, ZL)),
            dma((CHUNKS, NP)), dma((CHUNKS, NP)),
            dma((CHUNKS, NP)), dma((CHUNKS, NP)),
            dma,
        ],
        compiler_params=pltpu.CompilerParams(
            collective_id=0, has_side_effects=True, vmem_limit_bytes=40 * 2**20
        ),
        name="outer_step",
    )(
        tokens[0], up_values[0].T, out_grad[0].T, weights[0].T, momentum[0].T,
        path_table[:, 0], live_tokens,
    )
    return new.T[None]


def solution(mesh):
    return jax.shard_map(
        on_device,
        mesh=mesh,
        in_specs=(
            P("path", "fsdp", None),
            P("path", None, "fsdp"),
            P("path", None, "fsdp"),
            P("path", None, "fsdp"),
            P("path", None, "fsdp"),
            P(),
            P("path"),
        ),
        out_specs=P("path", None, "fsdp"),
        check_vma=False,
    )
```

```python
import jax
import jax.numpy as jnp
from jax import lax
from jax.experimental import pallas as pl
from jax.experimental.pallas import tpu as pltpu
from jax.sharding import PartitionSpec as P

MESH = pl.DeviceIdType.MESH

NX, ZH, NY, ZL = 4, 3, 8, 4
NP = NX * ZH
D, TOK, COLS = 4096, 1024, 120
ROWS = TOK // (NY * ZL * 2)
BUNDLE = ROWS * ZL * 2
QUARTER = D // NX
THIRD = COLS // ZH
CHUNKS = 2
LANES = 256
PART = THIRD * QUARTER // (CHUNKS * LANES)
SUBS = PART // THIRD

SLOT = {0: 0, 4: 1, 1: 2, -1: 3, 2: 4, -2: 5, 3: 6, -3: 7}
SPREAD = (0, 2, -2)
STEPS = (
    [(0, 1), (1, 0), (-1, 0), (0, 2), (2, 0), (-2, 0), (0, 3)]
    + [(1, 1), (-1, 1), (0,), (1, 2), (-1, 2), (2, 1), (-2, 1), (3, 0), (-3, 0), (1, 3), (-1, 3)]
    + [(2, 2), (-2, 2), ((1, -1),), (3, 1), (-3, 1), (2, 3), (-2, 3), (3, 2), (-3, 2), ((2, -2),)]
    + [(4, 0), (4, 1), (3, 3), (-3, 3), ((3, -3),), (4, 2), (4, 3)]
)
BLOCKS = [(0, 0)] + [step for step in STEPS if len(step) == 2]


def y_hops(rel, k):
    hops = []
    for way, after in ((0, rel - 1), (1, rel + 1)):
        if rel == 4 or (rel > 0) == (way == 0) and rel != 0:
            continue
        if abs(after) == 4:
            if (k < 2) == (way == 0):
                hops.append((way, 4))
        elif k == 0 or after not in SPREAD:
            hops.append((way, after))
    return hops


def body(
    tok_in, up_in, og_in, w_in, mom_in, table, live, out,
    tok, up, og, w, mom, acc, psend, precv, asend, arecv, fresh, share, inv,
    load_sem, own_sem, t_send, t_recv, c_send, c_recv,
    p_send, p_recv, a_send, a_recv, out_sem,
):
    path = lax.axis_index("path")
    fsdp = lax.axis_index("fsdp")
    core = fsdp % 2
    z = (fsdp // 2) % ZL
    y = fsdp // (2 * ZL)
    x = path // ZH
    third = path % ZH

    def at(yy, zz, cc):
        return (path, (yy * ZL + zz) * 2 + cc)

    order = (z, z + 1 - 2 * (z % 2), 2 - z // 2, 3 - 3 * (z // 2))
    up_y, down_y = at((y + 1) % NY, z, core), at((y + NY - 1) % NY, z, core)
    up_z, down_z = at(y, (z + 1) % ZL, core), at(y, (z + ZL - 1) % ZL, core)
    sibling = at(y, z, 1 - core)

    loads = [
        pltpu.make_async_copy(src, dst, load_sem.at[i])
        for i, (src, dst) in enumerate(((w_in, w), (up_in, up), (og_in, og), (mom_in, mom)))
    ]

    def rows(rel, k):
        return pl.ds(pl.multiple_of(SLOT[rel] * BUNDLE + (order[k] * 2 + core) * ROWS, ROWS), ROWS)

    own = pltpu.make_async_copy(tok_in, tok.at[rows(0, 0)], t_recv.at[SLOT[0], z])
    own.start()
    for load in loads:
        load.start()

    barrier = pltpu.get_barrier_semaphore()
    friends = [up_y, down_y, up_z, down_z, sibling]
    friends += [((path + o) % NP, fsdp) for o in range(1, NP)]
    for friend in friends:
        pl.semaphore_signal(barrier, inc=1, device_id=friend, device_id_type=MESH)
    pl.semaphore_wait(barrier, len(friends))

    def source(rel, k):
        return tok_in if rel == 0 and k == 0 else tok.at[rows(rel, k)]

    def t_copy(link, rel, k, after):
        return pltpu.make_async_remote_copy(
            src_ref=source(rel, k), dst_ref=tok.at[rows(after, k)],
            send_sem=t_send.at[link, SLOT[rel], order[k]], recv_sem=t_recv.at[SLOT[after], order[k]],
            device_id=(up_y, down_y, up_z, down_z)[link], device_id_type=MESH,
        )

    def c_copy(rel, k):
        return pltpu.make_async_remote_copy(
            src_ref=source(rel, k), dst_ref=tok.at[rows(rel, k)],
            send_sem=c_send.at[SLOT[rel], order[k]], recv_sem=c_recv.at[SLOT[rel], order[k]],
            device_id=sibling, device_id_type=MESH,
        )

    def for_hops(rel, k, act):
        for way, after in y_hops(rel, k):
            act(t_copy(way, rel, k, after))
        if rel in SPREAD:
            pl.when((order[k] <= z) & (z < ZL - 1))(lambda: act(t_copy(2, rel, k, rel)))
            pl.when((order[k] >= z) & (z > 0))(lambda: act(t_copy(3, rel, k, rel)))
        act(c_copy(rel, k))

    def gate_and_grad(rels, first):
        start, count = SLOT[rels[0]] * BUNDLE, len(rels) * BUNDLE
        gate = lax.dot_general(
            w[...], tok[start : start + count], (((1,), (1,)), ((), ())), preferred_element_type=jnp.float32
        ) * (1.0 / D**0.5)
        parts = []
        for i, rel in enumerate(rels):
            here = (y + rel + NY) % NY * BUNDLE
            lanes = pl.ds(pl.multiple_of(here, BUNDLE), BUNDLE)
            g = gate[:, i * BUNDLE : (i + 1) * BUNDLE]
            sig = jax.nn.sigmoid(g)
            slope = sig * (1.0 + g * (1.0 - sig))
            term = og[:, lanes].astype(jnp.float32) * up[:, lanes].astype(jnp.float32) * slope
            token = here + lax.broadcasted_iota(jnp.int32, (COLS, BUNDLE), 1)
            parts.append(jnp.where(token < live[0], term, 0.0).astype(jnp.bfloat16))
        return start, count, parts[0] if len(parts) == 1 else jnp.concatenate(parts, axis=1)

    def accumulate(rels, first):
        start, count, grad = gate_and_grad(rels, first)
        for q in range(NX):
            lanes = slice(q * QUARTER, (q + 1) * QUARTER)
            term = jnp.dot(grad, tok[start : start + count, lanes], preferred_element_type=jnp.float32)
            if first:
                acc[:, lanes] = term
            else:
                acc[:, lanes] += term

    def wait_sibling(rel):
        for k in range(ZL):
            c_copy(rel, k).wait_recv()

    for_hops(0, 0, lambda copy: copy.start())
    for g in range(NP):
        total = jnp.float32(0.0)
        for h in range(NP):
            same = jnp.where(table[g] == table[h], 1.0, 0.0).astype(jnp.float32)
            share[g * NP + h] = same
            total = total + same
        inv[g] = 1.0 / total
    own.wait()
    for load in loads[:3]:
        load.wait()
    for step in STEPS:
        if len(step) == 2:
            t_copy(0, step[0], step[1], step[0]).wait_recv()
            for_hops(*step, lambda copy: copy.start())
        else:
            rels = step[0] if isinstance(step[0], tuple) else step
            for rel in rels:
                wait_sibling(rel)
            accumulate(rels, rels == (0,))
    wait_sibling(4)

    def p_copy(chunk, dest):
        return pltpu.make_async_remote_copy(
            src_ref=psend.at[chunk, dest], dst_ref=precv.at[chunk, path],
            send_sem=p_send.at[chunk, dest], recv_sem=p_recv.at[chunk, path],
            device_id=(dest, fsdp), device_id_type=MESH,
        )

    def p_arrival(chunk, source):
        return pltpu.make_async_remote_copy(
            src_ref=psend.at[chunk, source], dst_ref=precv.at[chunk, source],
            send_sem=p_send.at[chunk, source], recv_sem=p_recv.at[chunk, source],
            device_id=(source, fsdp), device_id_type=MESH,
        )

    def a_copy(chunk, dest):
        return pltpu.make_async_remote_copy(
            src_ref=asend.at[chunk, dest], dst_ref=arecv.at[chunk, path],
            send_sem=a_send.at[chunk, dest], recv_sem=a_recv.at[chunk, path],
            device_id=(dest, fsdp), device_id_type=MESH,
        )

    def a_arrival(chunk, source):
        return pltpu.make_async_remote_copy(
            src_ref=asend.at[chunk, source], dst_ref=arecv.at[chunk, source],
            send_sem=a_send.at[chunk, source], recv_sem=a_recv.at[chunk, source],
            device_id=(source, fsdp), device_id_type=MESH,
        )

    start, count, grad = gate_and_grad((4,), False)
    for j in range(NX):
        q = (x + j) % NX
        lanes = pl.ds(pl.multiple_of(q * QUARTER, QUARTER), QUARTER)
        total = acc[:, lanes] + jnp.dot(grad, tok[start : start + count, lanes], preferred_element_type=jnp.float32)
        total = total * (1.0 / D**0.5)
        for chunk in range(CHUNKS):
            for i in range(ZH):
                r = (third + 1 + i) % ZH
                dest = q * ZH + r
                first = chunk * SUBS * LANES
                for rr in range(ZH):
                    piece = jnp.concatenate(
                        [
                            total[rr * THIRD : (rr + 1) * THIRD, first + s * LANES : first + (s + 1) * LANES]
                            for s in range(SUBS)
                        ],
                        axis=0,
                    ).astype(jnp.bfloat16)
                    if i == 0:
                        psend[chunk, q * ZH + rr] = piece
                if j > 0 or i < ZH - 1:
                    p_copy(chunk, dest).start()

    for chunk in range(CHUNKS):
        for o in range(1, NP):
            p_arrival(chunk, (path + o) % NP).wait_recv()
        mine = pltpu.make_async_copy(psend.at[chunk, path], precv.at[chunk, path], own_sem)
        mine.start()
        mine.wait()

        @pl.loop(0, PART // 16)
        def _(i):
            part = pl.ds(pl.multiple_of(i * 16, 16), 16)
            values = [precv[chunk, h, part].astype(jnp.float32) for h in range(NP)]
            for g in range(NP):
                total = share[g * NP] * values[0]
                for h in range(1, NP):
                    total = total + share[g * NP + h] * values[h]
                asend[chunk, g, part] = (total * inv[g]).astype(jnp.bfloat16)

        for o in range(1, NP):
            a_copy(chunk, (path + o) % NP).start()

    loads[3].wait()
    for chunk in range(CHUNKS):
        mine = pltpu.make_async_copy(asend.at[chunk, path], arecv.at[chunk, path], own_sem)
        mine.start()
        mine.wait()
        for o in range(1, NP):
            a_arrival(chunk, (path + o) % NP).wait_recv()
        for q in range(NX):
            for s in range(SUBS):
                lanes = slice(q * QUARTER + (chunk * SUBS + s) * LANES, q * QUARTER + (chunk * SUBS + s + 1) * LANES)
                averaged = jnp.concatenate(
                    [
                        arecv[chunk, q * ZH + r].astype(jnp.float32)[s * THIRD : (s + 1) * THIRD]
                        for r in range(ZH)
                    ],
                    axis=0,
                )
                moment = 0.9 * mom[:, lanes] + averaged
                new = w[:, lanes].astype(jnp.float32) - 0.7 * (averaged + 0.9 * moment)
                fresh[:, lanes] = new.astype(jnp.bfloat16)
    write = pltpu.make_async_copy(fresh, out, out_sem)
    write.start()

    for block in BLOCKS:
        for_hops(*block, lambda copy: copy.wait_send())
    for chunk in range(CHUNKS):
        for o in range(1, NP):
            p_copy(chunk, (path + o) % NP).wait_send()
            a_copy(chunk, (path + o) % NP).wait_send()
    write.wait()


def on_device(tokens, up_values, out_grad, weights, momentum, path_table, live_tokens):
    dma = pltpu.SemaphoreType.DMA
    bf16, f32 = jnp.bfloat16, jnp.float32
    anywhere = pl.BlockSpec(memory_space=pl.ANY)
    scalars = pl.BlockSpec(memory_space=pltpu.SMEM)
    shard = pltpu.VMEM((CHUNKS, NP, PART, LANES), bf16)
    new = pl.pallas_call(
        body,
        out_shape=jax.ShapeDtypeStruct((COLS, D), bf16),
        in_specs=[anywhere] * 5 + [scalars] * 2,
        out_specs=anywhere,
        scratch_shapes=[
            pltpu.VMEM((TOK, D), bf16),
            pltpu.VMEM((COLS, TOK), bf16),
            pltpu.VMEM((COLS, TOK), bf16),
            pltpu.VMEM((COLS, D), bf16),
            pltpu.VMEM((COLS, D), f32),
            pltpu.VMEM((COLS, D), f32),
            shard, shard, shard, shard,
            pltpu.VMEM((COLS, D), bf16),
            pltpu.SMEM((NP * NP,), f32),
            pltpu.SMEM((NP,), f32),
            dma((4,)),
            dma,
            dma((4, NY, ZL)), dma((NY, ZL)),
            dma((NY, ZL)), dma((NY, ZL)),
            dma((CHUNKS, NP)), dma((CHUNKS, NP)),
            dma((CHUNKS, NP)), dma((CHUNKS, NP)),
            dma,
        ],
        compiler_params=pltpu.CompilerParams(
            collective_id=0, has_side_effects=True, vmem_limit_bytes=62 * 2**20
        ),
        name="outer_step",
    )(
        tokens[0], up_values[0].T, out_grad[0].T, weights[0].T, momentum[0].T,
        path_table[:, 0], live_tokens,
    )
    return new.T[None]


def solution(mesh):
    return jax.shard_map(
        on_device,
        mesh=mesh,
        in_specs=(
            P("path", "fsdp", None),
            P("path", None, "fsdp"),
            P("path", None, "fsdp"),
            P("path", None, "fsdp"),
            P("path", None, "fsdp"),
            P(),
            P("path"),
        ),
        out_specs=P("path", None, "fsdp"),
        check_vma=False,
    )
```

```python
import functools

import jax
import jax.numpy as jnp
from jax import lax
from jax.experimental import pallas as pl
from jax.experimental.pallas import tpu as pltpu
from jax.sharding import PartitionSpec as P

MESH = pl.DeviceIdType.MESH

NX, ZH, NY, ZL = 4, 3, 8, 4
NP = NX * ZH
D, TOK, COLS = 4096, 1024, 120
ROWS = TOK // (NY * ZL * 2)
BUNDLE = ROWS * ZL * 2
QUARTER = D // NX
THIRD = COLS // ZH
SLOT = {0: 0, 4: 1, 1: 2, -1: 3, 2: 4, -2: 5, 3: 6, -3: 7}
SPREAD = (0, 2, -2)
STEPS = (
    [(0, 1), (1, 0), (-1, 0), (0, 2), (2, 0), (-2, 0), (0, 3)]
    + [(1, 1), (-1, 1), (0,), (1, 2), (-1, 2), (2, 1), (-2, 1), (3, 0), (-3, 0), (1, 3), (-1, 3)]
    + [(2, 2), (-2, 2), ((1, -1),), (3, 1), (-3, 1), (2, 3), (-2, 3), (3, 2), (-3, 2), ((2, -2),)]
    + [(4, 0), (4, 1), (3, 3), (-3, 3), ((3, -3),), (4, 2), (4, 3)]
)
BLOCKS = [(0, 0)] + [step for step in STEPS if len(step) == 2]


def y_hops(rel, k):
    hops = []
    for way, after in ((0, rel - 1), (1, rel + 1)):
        if rel == 4 or (rel > 0) == (way == 0) and rel != 0:
            continue
        if abs(after) == 4:
            if (k < 2) == (way == 0):
                hops.append((way, 4))
        elif k == 0 or after not in SPREAD:
            hops.append((way, after))
    return hops


def body(
    slots, chunks, lanes_of, tok_in, up_in, og_in, w_in, mom_in, table, live, out,
    tok, up, og, w, mom, acc, psend, precv, asend, arecv, zbuf, fresh, share, inv, module,
    load_sem, own_sem, t_send, t_recv, c_send, c_recv,
    p_send, p_recv, a_send, a_recv, z_send, z_recv, out_sem,
):
    part_rows = THIRD * QUARTER // (chunks * lanes_of)
    subs = part_rows // THIRD
    width = subs * lanes_of
    path = lax.axis_index("path")
    fsdp = lax.axis_index("fsdp")
    core = fsdp % 2
    z = (fsdp // 2) % ZL
    y = fsdp // (2 * ZL)
    x = path // ZH
    third = path % ZH

    def at(yy, zz, cc):
        return (path, (yy * ZL + zz) * 2 + cc)

    order = (z, z + 1 - 2 * (z % 2), 2 - z // 2, 3 - 3 * (z // 2))
    up_y, down_y = at((y + 1) % NY, z, core), at((y + NY - 1) % NY, z, core)
    up_z, down_z = at(y, (z + 1) % ZL, core), at(y, (z + ZL - 1) % ZL, core)
    sibling = at(y, z, 1 - core)

    loads = [
        pltpu.make_async_copy(src, dst, load_sem.at[i])
        for i, (src, dst) in enumerate(((w_in, w), (up_in, up), (og_in, og), (mom_in, mom)))
    ]

    def rows(rel, k):
        return pl.ds(pl.multiple_of(SLOT[rel] * BUNDLE + (order[k] * 2 + core) * ROWS, ROWS), ROWS)

    own = pltpu.make_async_copy(tok_in, tok.at[rows(0, 0)], t_recv.at[SLOT[0], z])
    own.start()
    for load in loads:
        load.start()

    barrier = pltpu.get_barrier_semaphore()
    friends = [up_y, down_y, up_z, down_z, sibling]
    if slots is None:
        friends += [((path + o) % NP, fsdp) for o in range(1, NP)]
    else:
        friends += [((x + o) % NX * ZH + third, fsdp) for o in range(1, NX)]
        friends += [(x * ZH + (third + o) % ZH, fsdp) for o in range(1, ZH)]
    for friend in friends:
        pl.semaphore_signal(barrier, inc=1, device_id=friend, device_id_type=MESH)
    pl.semaphore_wait(barrier, len(friends))

    def source(rel, k):
        return tok_in if rel == 0 and k == 0 else tok.at[rows(rel, k)]

    def t_copy(link, rel, k, after):
        return pltpu.make_async_remote_copy(
            src_ref=source(rel, k), dst_ref=tok.at[rows(after, k)],
            send_sem=t_send.at[link, SLOT[rel], order[k]], recv_sem=t_recv.at[SLOT[after], order[k]],
            device_id=(up_y, down_y, up_z, down_z)[link], device_id_type=MESH,
        )

    def c_copy(rel, k):
        return pltpu.make_async_remote_copy(
            src_ref=source(rel, k), dst_ref=tok.at[rows(rel, k)],
            send_sem=c_send.at[SLOT[rel], order[k]], recv_sem=c_recv.at[SLOT[rel], order[k]],
            device_id=sibling, device_id_type=MESH,
        )

    def for_hops(rel, k, act):
        for way, after in y_hops(rel, k):
            act(t_copy(way, rel, k, after))
        if rel in SPREAD:
            pl.when((order[k] <= z) & (z < ZL - 1))(lambda: act(t_copy(2, rel, k, rel)))
            pl.when((order[k] >= z) & (z > 0))(lambda: act(t_copy(3, rel, k, rel)))
        act(c_copy(rel, k))

    def gate_and_grad(rels, first):
        start, count = SLOT[rels[0]] * BUNDLE, len(rels) * BUNDLE
        gate = lax.dot_general(
            w[...], tok[start : start + count], (((1,), (1,)), ((), ())), preferred_element_type=jnp.float32
        ) * (1.0 / D**0.5)
        parts = []
        for i, rel in enumerate(rels):
            here = (y + rel + NY) % NY * BUNDLE
            lanes = pl.ds(pl.multiple_of(here, BUNDLE), BUNDLE)
            g = gate[:, i * BUNDLE : (i + 1) * BUNDLE]
            sig = jax.nn.sigmoid(g)
            slope = sig * (1.0 + g * (1.0 - sig))
            term = og[:, lanes].astype(jnp.float32) * up[:, lanes].astype(jnp.float32) * slope
            token = here + lax.broadcasted_iota(jnp.int32, (COLS, BUNDLE), 1)
            parts.append(jnp.where(token < live[0], term, 0.0).astype(jnp.bfloat16))
        return start, count, parts[0] if len(parts) == 1 else jnp.concatenate(parts, axis=1)

    def accumulate(rels, first):
        start, count, grad = gate_and_grad(rels, first)
        for q in range(NX):
            lanes = slice(q * QUARTER, (q + 1) * QUARTER)
            term = jnp.dot(grad, tok[start : start + count, lanes], preferred_element_type=jnp.float32)
            if first:
                acc[:, lanes] = term
            else:
                acc[:, lanes] += term

    def wait_sibling(rel):
        for k in range(ZL):
            c_copy(rel, k).wait_recv()

    for_hops(0, 0, lambda copy: copy.start())
    def one_if(condition):
        return jnp.where(condition, 1.0, 0.0).astype(jnp.float32)

    def members(name):
        return functools.reduce(lambda a, b: a + b, [one_if(table[h] == name) for h in range(NP)])

    if slots is None:
        for g in range(NP):
            for h in range(NP):
                share[g * NP + h] = one_if(table[g] == table[h])
            inv[g] = 1.0 / members(table[g])
    else:
        for r in range(ZH):
            names = [-1 - r * slots - j for j in range(slots)]
            taken = jnp.int32(0)
            for xx in range(NX):
                name = table[xx * ZH + r]
                abroad = functools.reduce(
                    jnp.logical_or, [table[g] == name for g in range(NP) if g % ZH != r]
                )
                fresh_name = abroad
                for before in range(xx):
                    fresh_name = fresh_name & (table[before * ZH + r] != name)
                names = [jnp.where(fresh_name & (taken == j), name, old) for j, old in enumerate(names)]
                taken = taken + jnp.where(fresh_name, 1, 0)
            for j in range(slots):
                module[r * slots + j] = names[j]
        mine = [table[xx * ZH + third] for xx in range(NX)]
        planes = [(third + o) % ZH for o in range(1, ZH)]
        here = [module[third * slots + j] for j in range(slots)]
        there = [[module[r * slots + j] for j in range(slots)] for r in planes]
        count = 0

        def keep(values):
            nonlocal count
            at_ = count
            for value in values:
                share[count] = value
                count += 1
            return [share[at_ + i] for i in range(len(values))]

        partial_of = [keep([one_if(name == here[j]) for name in mine]) for j in range(slots)]

        def total_of(wanted):
            scale = 1.0 / jnp.maximum(members(wanted), 1.0)
            terms = [one_if(name == wanted) for name in mine]
            terms += [one_if(name == wanted) for names in there for name in names]
            return keep([term * scale for term in terms])

        totals_of = [[total_of(there[i][j]) for j in range(slots)] for i in range(ZH - 1)]
        averages_of = [total_of(mine[g]) for g in range(NX)]
        spread_of = []
        for g in range(NX):
            picks = [one_if(mine[g] == here[j]) for j in range(slots)]
            alone = 1.0 - functools.reduce(lambda a, b: a + b, picks)
            scale = alone / members(mine[g])
            spread_of.append(keep(picks + [one_if(name == mine[g]) * scale for name in mine]))
    own.wait()
    for load in loads[:3]:
        load.wait()
    for step in STEPS:
        if len(step) == 2:
            t_copy(0, step[0], step[1], step[0]).wait_recv()
            for_hops(*step, lambda copy: copy.start())
        else:
            rels = step[0] if isinstance(step[0], tuple) else step
            for rel in rels:
                wait_sibling(rel)
            accumulate(rels, rels == (0,))
    wait_sibling(4)

    def remote(src, dst, send_sem, recv_sem, to):
        return pltpu.make_async_remote_copy(
            src_ref=src, dst_ref=dst, send_sem=send_sem, recv_sem=recv_sem, device_id=(to, fsdp), device_id_type=MESH
        )

    def p_copy(chunk, dest):
        return remote(
            psend.at[chunk, dest], precv.at[chunk, path], p_send.at[chunk, dest], p_recv.at[chunk, path], dest
        )

    def p_arrival(chunk, source):
        return remote(
            psend.at[chunk, source], precv.at[chunk, source], p_send.at[chunk, source], p_recv.at[chunk, source], source
        )

    def a_copy(chunk, dest):
        return remote(
            asend.at[chunk, dest], arecv.at[chunk, path], a_send.at[chunk, dest], a_recv.at[chunk, path], dest
        )

    def a_arrival(chunk, source):
        return remote(
            asend.at[chunk, source], arecv.at[chunk, source], a_send.at[chunk, source], a_recv.at[chunk, source], source
        )

    def of_x(xx):
        return pl.ds(xx * ZH, ZH)

    def x_copy(back, chunk, dest, landing):
        out_buf, in_buf, out_sem_, in_sem = ((psend, precv, p_send, p_recv), (asend, arecv, a_send, a_recv))[back]
        return remote(
            out_buf.at[chunk, of_x(dest)], in_buf.at[chunk, of_x(landing)],
            out_sem_.at[chunk, dest], in_sem.at[chunk, landing], dest * ZH + third,
        )

    def z_copy(back, chunk, o):
        return remote(
            zbuf.at[2 * back, chunk, o - 1], zbuf.at[2 * back + 1, chunk, ZH - 1 - o],
            z_send.at[back, chunk, o - 1], z_recv.at[back, chunk, ZH - 1 - o],
            x * ZH + (third + o) % ZH,
        )

    start, count, grad = gate_and_grad((4,), False)

    def last_products(chunk):
        for j in (1, 2, 3, 0):
            q = (x + j) % NX
            first = pl.multiple_of(q * QUARTER + chunk * width, width)
            lanes = pl.ds(first, width)
            total = acc[:, lanes] + jnp.dot(
                grad, tok[start : start + count, lanes], preferred_element_type=jnp.float32
            )
            total = total * (1.0 / D**0.5)
            for r in range(ZH):
                piece = jnp.concatenate(
                    [
                        total[r * THIRD : (r + 1) * THIRD, s * lanes_of : (s + 1) * lanes_of]
                        for s in range(subs)
                    ],
                    axis=0,
                ).astype(jnp.bfloat16)
                if slots is not None and j == 0:
                    precv[chunk, q * ZH + r] = piece
                else:
                    psend[chunk, q * ZH + r] = piece
            if slots is None:
                for i in range(ZH - 1 if j == 0 else ZH):
                    p_copy(chunk, q * ZH + (third + 1 + i) % ZH).start()
            elif j > 0 and chunk == 0:
                x_copy(0, chunk, q, x).start()

    for chunk in range(chunks):
        last_products(chunk)
    if slots is not None:
        for o in range(1, NX):
            x_copy(0, 1, (x + o) % NX, x).start()

    def combine(coefficients, values):
        total = coefficients[0] * values[0]
        for c, v in zip(coefficients[1:], values[1:]):
            total = total + c * v
        return total

    def row_tiles(work):
        @pl.loop(0, part_rows // 16)
        def _(i):
            work(pl.ds(pl.multiple_of(i * 16, 16), 16))

    def f32(value):
        return value.astype(jnp.float32)

    def own_copy(chunk):
        if slots is None:
            return pltpu.make_async_copy(asend.at[chunk, path], arecv.at[chunk, path], own_sem.at[chunk])
        return pltpu.make_async_copy(asend.at[chunk, of_x(x)], arecv.at[chunk, of_x(x)], own_sem.at[chunk])

    def own_average(chunk):
        for o in range(1, NP):
            p_arrival(chunk, (path + o) % NP).wait_recv()
        mine_ = pltpu.make_async_copy(psend.at[chunk, path], precv.at[chunk, path], own_sem.at[chunk])
        mine_.start()
        mine_.wait()

        def work(part):
            values = [f32(precv[chunk, h, part]) for h in range(NP)]
            for g in range(NP):
                total = combine([share[g * NP + h] for h in range(NP)], values)
                asend[chunk, g, part] = (total * inv[g]).astype(jnp.bfloat16)

        row_tiles(work)
        own_copy(chunk).start()
        for o in range(1, NP):
            a_copy(chunk, (path + o) % NP).start()

    def partial_sums(chunk):
        for o in range(1, NX):
            x_copy(0, chunk, (x + o) % NX, (x + o) % NX).wait_recv()
        if chunk + 2 < chunks:
            for o in range(1, NX):
                x_copy(0, chunk + 2, (x + o) % NX, x).start()

        def work(part):
            for i, r in enumerate(planes):
                values = [f32(precv[chunk, g * ZH + r, part]) for g in range(NX)]
                for j in range(slots):
                    zbuf[0, chunk, i, j, part] = combine(partial_of[j], values).astype(jnp.bfloat16)

        row_tiles(work)
        for o in range(1, ZH):
            z_copy(0, chunk, o).start()

    def totals(chunk):
        for o in range(1, ZH):
            z_copy(0, chunk, o).wait_recv()

        def work(part):
            values = [f32(precv[chunk, g * ZH + third, part]) for g in range(NX)]
            values += [f32(zbuf[1, chunk, i, j, part]) for i in range(ZH - 1) for j in range(slots)]
            for i in range(ZH - 1):
                for j in range(slots):
                    zbuf[2, chunk, i, j, part] = combine(totals_of[i][j], values).astype(jnp.bfloat16)
            for g in range(NX):
                asend[chunk, g * ZH + third, part] = combine(averages_of[g], values).astype(jnp.bfloat16)

        row_tiles(work)
        for o in range(1, ZH):
            z_copy(1, chunk, o).start()

    def spread(chunk):
        for o in range(1, ZH):
            z_copy(1, chunk, o).wait_recv()

        def work(part):
            for i, r in enumerate(planes):
                values = [f32(zbuf[3, chunk, i, j, part]) for j in range(slots)]
                values += [f32(precv[chunk, g * ZH + r, part]) for g in range(NX)]
                for g in range(NX):
                    asend[chunk, g * ZH + r, part] = combine(spread_of[g], values).astype(jnp.bfloat16)

        row_tiles(work)
        for o in range(1, NX):
            x_copy(1, chunk, (x + o) % NX, x).start()
        own_copy(chunk).start()

    def write(chunk, q):
        lanes = slice(q * QUARTER + chunk * width, q * QUARTER + (chunk + 1) * width)
        return pltpu.make_async_copy(fresh.at[:, lanes], out.at[:, lanes], out_sem.at[chunk, q])

    def update(chunk):
        own_copy(chunk).wait()
        if slots is None:
            for o in range(1, NP):
                a_arrival(chunk, (path + o) % NP).wait_recv()
        else:
            for o in range(1, NX):
                x_copy(1, chunk, (x + o) % NX, (x + o) % NX).wait_recv()
        for q in range(NX):
            for s in range(subs):
                first = q * QUARTER + chunk * width + s * lanes_of
                lanes = slice(first, first + lanes_of)
                averaged = jnp.concatenate(
                    [
                        arecv[chunk, q * ZH + r].astype(jnp.float32)[s * THIRD : (s + 1) * THIRD]
                        for r in range(ZH)
                    ],
                    axis=0,
                )
                moment = 0.9 * mom[:, lanes] + averaged
                new = w[:, lanes].astype(jnp.float32) - 0.7 * (averaged + 0.9 * moment)
                fresh[:, lanes] = new.astype(jnp.bfloat16)
            write(chunk, q).start()

    loads[3].wait()
    if slots is None:
        for chunk in range(chunks):
            own_average(chunk)
        for chunk in range(chunks):
            update(chunk)
    else:
        for chunk in range(chunks):
            partial_sums(chunk)
        for step in range(chunks + 2):
            for late, act in ((0, totals), (1, spread), (2, update)):
                if 0 <= step - late < chunks:
                    act(step - late)

    for block in BLOCKS:
        for_hops(*block, lambda copy: copy.wait_send())
    for chunk in range(chunks):
        if slots is None:
            for o in range(1, NP):
                p_copy(chunk, (path + o) % NP).wait_send()
                a_copy(chunk, (path + o) % NP).wait_send()
        else:
            for back in (0, 1):
                for o in range(1, NX):
                    x_copy(back, chunk, (x + o) % NX, x).wait_send()
                for o in range(1, ZH):
                    z_copy(back, chunk, o).wait_send()
    for chunk in range(chunks):
        for q in range(NX):
            write(chunk, q).wait()


def outer_step(slots, number, *arrays):
    dma = pltpu.SemaphoreType.DMA
    bf16, f32 = jnp.bfloat16, jnp.float32
    anywhere = pl.BlockSpec(memory_space=pl.ANY)
    scalars = pl.BlockSpec(memory_space=pltpu.SMEM)
    chunks, lanes_of = (2, 256) if slots is None else (4, 128)
    part_rows = THIRD * QUARTER // (chunks * lanes_of)
    shard = pltpu.VMEM((chunks, NP, part_rows, lanes_of), bf16)
    return pl.pallas_call(
        functools.partial(body, slots, chunks, lanes_of),
        out_shape=jax.ShapeDtypeStruct((COLS, D), bf16),
        in_specs=[anywhere] * 5 + [scalars] * 2,
        out_specs=anywhere,
        scratch_shapes=[
            pltpu.VMEM((TOK, D), bf16),
            pltpu.VMEM((COLS, TOK), bf16),
            pltpu.VMEM((COLS, TOK), bf16),
            pltpu.VMEM((COLS, D), bf16),
            pltpu.VMEM((COLS, D), f32),
            pltpu.VMEM((COLS, D), f32),
            shard, shard, shard, shard,
            pltpu.VMEM((4, chunks, ZH - 1, slots or 1, part_rows, lanes_of), bf16),
            pltpu.VMEM((COLS, D), bf16),
            pltpu.SMEM((NP * NP,), f32),
            pltpu.SMEM((NP,), f32),
            pltpu.SMEM((NP,), jnp.int32),
            dma((4,)),
            dma((chunks,)),
            dma((4, NY, ZL)), dma((NY, ZL)),
            dma((NY, ZL)), dma((NY, ZL)),
            dma((chunks, NP)), dma((chunks, NP)),
            dma((chunks, NP)), dma((chunks, NP)),
            dma((2, chunks, ZH - 1)), dma((2, chunks, ZH - 1)),
            dma((chunks, NX)),
        ],
        compiler_params=pltpu.CompilerParams(
            collective_id=number, has_side_effects=True, vmem_limit_bytes=62 * 2**20
        ),
        name="outer_step",
    )(*arrays)


def widest_plane(table, most):
    result = jnp.int32(0)
    for r in range(ZH):
        shared = jnp.int32(0)
        for xx in range(NX):
            name = table[xx * ZH + r]
            counts = functools.reduce(jnp.logical_or, [table[g] == name for g in range(NP) if g % ZH != r])
            for before in range(xx):
                counts = counts & (table[before * ZH + r] != name)
            shared = shared + jnp.where(counts, 1, 0)
        result = jnp.maximum(result, shared)
    most[0] = jnp.maximum(result, 2) - 2


def on_device(tokens, up_values, out_grad, weights, momentum, path_table, live_tokens):
    scalars = pl.BlockSpec(memory_space=pltpu.SMEM)
    table = path_table[:, 0]
    most = pl.pallas_call(
        widest_plane, out_shape=jax.ShapeDtypeStruct((1,), jnp.int32),
        in_specs=[scalars], out_specs=scalars, name="widest_plane",
    )(table)[0]
    arrays = (tokens[0], up_values[0].T, out_grad[0].T, weights[0].T, momentum[0].T, table, live_tokens)
    new = lax.switch(
        most,
        [functools.partial(outer_step, slots, number) for number, slots in enumerate((2, 3, None))],
        *arrays,
    )
    return new.T[None]


def solution(mesh):
    return jax.shard_map(
        on_device,
        mesh=mesh,
        in_specs=(
            P("path", "fsdp", None),
            P("path", None, "fsdp"),
            P("path", None, "fsdp"),
            P("path", None, "fsdp"),
            P("path", None, "fsdp"),
            P(),
            P("path"),
        ),
        out_specs=P("path", None, "fsdp"),
        check_vma=False,
    )
```

```python
import functools

import jax
import jax.numpy as jnp
from jax import lax
from jax.experimental import pallas as pl
from jax.experimental.pallas import tpu as pltpu
from jax.sharding import PartitionSpec as P

MESH = pl.DeviceIdType.MESH

NX, ZH, NY, ZL = 4, 3, 8, 4
NP = NX * ZH
D, TOK, COLS = 4096, 1024, 120
ROWS = TOK // (NY * ZL * 2)
BUNDLE = ROWS * ZL * 2
QUARTER = D // NX
THIRD = COLS // ZH
SLOT = {0: 0, 4: 1, 1: 2, -1: 3, 2: 4, -2: 5, 3: 6, -3: 7}
SPREAD = (0, 2, -2)
STEPS = (
    [(0, 1), (1, 0), (-1, 0), (0, 2), (2, 0), (-2, 0), (0, 3)]
    + [(1, 1), (-1, 1), (0,), (1, 2), (-1, 2), (2, 1), (-2, 1), (3, 0), (-3, 0), (1, 3), (-1, 3)]
    + [(2, 2), (-2, 2), ((1, -1),), (3, 1), (-3, 1), (2, 3), (-2, 3), (3, 2), (-3, 2), ((2, -2),)]
    + [(4, 0), (4, 1), (3, 3), (-3, 3), ((3, -3),), (4, 2), (4, 3)]
)
BLOCKS = [(0, 0)] + [step for step in STEPS if len(step) == 2]


def y_hops(rel, k):
    hops = []
    for way, after in ((0, rel - 1), (1, rel + 1)):
        if rel == 4 or (rel > 0) == (way == 0) and rel != 0:
            continue
        if abs(after) == 4:
            if (k < 2) == (way == 0):
                hops.append((way, 4))
        elif k == 0 or after not in SPREAD:
            hops.append((way, after))
    return hops


def body(
    slots, chunks, lanes_of, tok_in, up_in, og_in, w_in, mom_in, table, live, out,
    tok, up, og, w, mom, acc, psend, precv, asend, arecv, zbuf, fresh, share, inv, module,
    load_sem, own_sem, t_send, t_recv, c_send, c_recv,
    p_send, p_recv, a_send, a_recv, z_send, z_recv, out_sem,
):
    part_rows = THIRD * QUARTER // (chunks * lanes_of)
    subs = part_rows // THIRD
    width = subs * lanes_of
    path = lax.axis_index("path")
    fsdp = lax.axis_index("fsdp")
    core = fsdp % 2
    z = (fsdp // 2) % ZL
    y = fsdp // (2 * ZL)
    x = path // ZH
    third = path % ZH

    def at(yy, zz, cc):
        return (path, (yy * ZL + zz) * 2 + cc)

    order = (z, z + 1 - 2 * (z % 2), 2 - z // 2, 3 - 3 * (z // 2))
    up_y, down_y = at((y + 1) % NY, z, core), at((y + NY - 1) % NY, z, core)
    up_z, down_z = at(y, (z + 1) % ZL, core), at(y, (z + ZL - 1) % ZL, core)
    sibling = at(y, z, 1 - core)

    loads = [
        pltpu.make_async_copy(src, dst, load_sem.at[i])
        for i, (src, dst) in enumerate(((w_in, w), (up_in, up), (og_in, og), (mom_in, mom)))
    ]

    def rows(rel, k):
        return pl.ds(pl.multiple_of(SLOT[rel] * BUNDLE + (order[k] * 2 + core) * ROWS, ROWS), ROWS)

    own = pltpu.make_async_copy(tok_in, tok.at[rows(0, 0)], t_recv.at[SLOT[0], z])
    own.start()
    for load in loads:
        load.start()

    barrier = pltpu.get_barrier_semaphore()
    friends = [up_y, down_y, up_z, down_z, sibling]
    if slots is None:
        friends += [((path + o) % NP, fsdp) for o in range(1, NP)]
    else:
        friends += [((x + o) % NX * ZH + third, fsdp) for o in range(1, NX)]
        friends += [(x * ZH + (third + o) % ZH, fsdp) for o in range(1, ZH)]
    for friend in friends:
        pl.semaphore_signal(barrier, inc=1, device_id=friend, device_id_type=MESH)
    pl.semaphore_wait(barrier, len(friends))

    def source(rel, k):
        return tok_in if rel == 0 and k == 0 else tok.at[rows(rel, k)]

    def t_copy(link, rel, k, after):
        return pltpu.make_async_remote_copy(
            src_ref=source(rel, k), dst_ref=tok.at[rows(after, k)],
            send_sem=t_send.at[link, SLOT[rel], order[k]], recv_sem=t_recv.at[SLOT[after], order[k]],
            device_id=(up_y, down_y, up_z, down_z)[link], device_id_type=MESH,
        )

    def c_copy(rel, k):
        return pltpu.make_async_remote_copy(
            src_ref=source(rel, k), dst_ref=tok.at[rows(rel, k)],
            send_sem=c_send.at[SLOT[rel], order[k]], recv_sem=c_recv.at[SLOT[rel], order[k]],
            device_id=sibling, device_id_type=MESH,
        )

    def for_hops(rel, k, act):
        for way, after in y_hops(rel, k):
            act(t_copy(way, rel, k, after))
        if rel in SPREAD:
            pl.when((order[k] <= z) & (z < ZL - 1))(lambda: act(t_copy(2, rel, k, rel)))
            pl.when((order[k] >= z) & (z > 0))(lambda: act(t_copy(3, rel, k, rel)))
        act(c_copy(rel, k))

    def gate_and_grad(rels, first):
        start, count = SLOT[rels[0]] * BUNDLE, len(rels) * BUNDLE
        gate = lax.dot_general(
            w[...], tok[start : start + count], (((1,), (1,)), ((), ())), preferred_element_type=jnp.float32
        ) * (1.0 / D**0.5)
        parts = []
        for i, rel in enumerate(rels):
            here = (y + rel + NY) % NY * BUNDLE
            lanes = pl.ds(pl.multiple_of(here, BUNDLE), BUNDLE)
            g = gate[:, i * BUNDLE : (i + 1) * BUNDLE]
            sig = jax.nn.sigmoid(g)
            slope = sig * (1.0 + g * (1.0 - sig))
            term = og[:, lanes].astype(jnp.float32) * up[:, lanes].astype(jnp.float32) * slope
            token = here + lax.broadcasted_iota(jnp.int32, (COLS, BUNDLE), 1)
            parts.append(jnp.where(token < live[0], term, 0.0).astype(jnp.bfloat16))
        return start, count, parts[0] if len(parts) == 1 else jnp.concatenate(parts, axis=1)

    def accumulate(rels, first):
        start, count, grad = gate_and_grad(rels, first)
        for q in range(NX):
            lanes = slice(q * QUARTER, (q + 1) * QUARTER)
            term = jnp.dot(grad, tok[start : start + count, lanes], preferred_element_type=jnp.float32)
            if first:
                acc[:, lanes] = term
            else:
                acc[:, lanes] += term

    def wait_sibling(rel):
        for k in range(ZL):
            c_copy(rel, k).wait_recv()

    for_hops(0, 0, lambda copy: copy.start())
    def one_if(condition):
        return jnp.where(condition, 1.0, 0.0).astype(jnp.float32)

    def members(name):
        return functools.reduce(lambda a, b: a + b, [one_if(table[h] == name) for h in range(NP)])

    if slots is None:
        for g in range(NP):
            for h in range(NP):
                share[g * NP + h] = one_if(table[g] == table[h])
            inv[g] = 1.0 / members(table[g])
    else:
        for r in range(ZH):
            names = [-1 - r * slots - j for j in range(slots)]
            taken = jnp.int32(0)
            for xx in range(NX):
                name = table[xx * ZH + r]
                abroad = functools.reduce(
                    jnp.logical_or, [table[g] == name for g in range(NP) if g % ZH != r]
                )
                fresh_name = abroad
                for before in range(xx):
                    fresh_name = fresh_name & (table[before * ZH + r] != name)
                names = [jnp.where(fresh_name & (taken == j), name, old) for j, old in enumerate(names)]
                taken = taken + jnp.where(fresh_name, 1, 0)
            for j in range(slots):
                module[r * slots + j] = names[j]
        mine = [table[xx * ZH + third] for xx in range(NX)]
        planes = [(third + o) % ZH for o in range(1, ZH)]
        here = [module[third * slots + j] for j in range(slots)]
        there = [[module[r * slots + j] for j in range(slots)] for r in planes]
        count = 0

        def keep(values):
            nonlocal count
            at_ = count
            for value in values:
                share[count] = value
                count += 1
            return [share[at_ + i] for i in range(len(values))]

        partial_of = [keep([one_if(name == here[j]) for name in mine]) for j in range(slots)]

        def total_of(wanted):
            scale = 1.0 / jnp.maximum(members(wanted), 1.0)
            terms = [one_if(name == wanted) for name in mine]
            terms += [one_if(name == wanted) for names in there for name in names]
            return keep([term * scale for term in terms])

        totals_of = [[total_of(there[i][j]) for j in range(slots)] for i in range(ZH - 1)]
        averages_of = [total_of(mine[g]) for g in range(NX)]
        spread_of = []
        for g in range(NX):
            picks = [one_if(mine[g] == here[j]) for j in range(slots)]
            alone = 1.0 - functools.reduce(lambda a, b: a + b, picks)
            scale = alone / members(mine[g])
            spread_of.append(keep(picks + [one_if(name == mine[g]) * scale for name in mine]))
    own.wait()
    for load in loads[:3]:
        load.wait()
    for step in STEPS:
        if len(step) == 2:
            t_copy(0, step[0], step[1], step[0]).wait_recv()
            for_hops(*step, lambda copy: copy.start())
        else:
            rels = step[0] if isinstance(step[0], tuple) else step
            for rel in rels:
                wait_sibling(rel)
            accumulate(rels, rels == (0,))
    wait_sibling(4)

    def remote(src, dst, send_sem, recv_sem, to):
        return pltpu.make_async_remote_copy(
            src_ref=src, dst_ref=dst, send_sem=send_sem, recv_sem=recv_sem, device_id=(to, fsdp), device_id_type=MESH
        )

    def p_copy(chunk, dest):
        return remote(
            psend.at[chunk, dest], precv.at[chunk, path], p_send.at[chunk, dest], p_recv.at[chunk, path], dest
        )

    def p_arrival(chunk, source):
        return remote(
            psend.at[chunk, source], precv.at[chunk, source], p_send.at[chunk, source], p_recv.at[chunk, source], source
        )

    def a_copy(chunk, dest):
        return remote(
            asend.at[chunk, dest], arecv.at[chunk, path], a_send.at[chunk, dest], a_recv.at[chunk, path], dest
        )

    def a_arrival(chunk, source):
        return remote(
            asend.at[chunk, source], arecv.at[chunk, source], a_send.at[chunk, source], a_recv.at[chunk, source], source
        )

    def turned(r):
        return (r - third + ZH) % ZH

    def of_x(xx):
        return pl.ds(xx * ZH, ZH)

    def x_copy(back, chunk, dest, landing, others):
        def of(xx):
            return pl.ds(xx * ZH + 1, ZH - 1) if others else pl.ds(xx * ZH, 1)

        out_buf, in_buf, out_sem_, in_sem = ((psend, precv, p_send, p_recv), (asend, arecv, a_send, a_recv))[back]
        return remote(
            out_buf.at[chunk, of(dest)], in_buf.at[chunk, of(landing)],
            out_sem_.at[chunk, others * NX + dest], in_sem.at[chunk, others * NX + landing], dest * ZH + third,
        )

    def x_start(back, chunk, others):
        for o in range(1, NX):
            x_copy(back, chunk, (x + o) % NX, x, others).start()

    def x_wait(back, chunk, others):
        for o in range(1, NX):
            x_copy(back, chunk, (x + o) % NX, (x + o) % NX, others).wait_recv()

    def z_copy(back, chunk, o):
        return remote(
            zbuf.at[2 * back, chunk, o - 1], zbuf.at[2 * back + 1, chunk, ZH - 1 - o],
            z_send.at[back, chunk, o - 1], z_recv.at[back, chunk, ZH - 1 - o],
            x * ZH + (third + o) % ZH,
        )

    start, count, grad = gate_and_grad((4,), False)

    def last_products(chunk):
        for j in (1, 2, 3, 0):
            q = (x + j) % NX
            first = pl.multiple_of(q * QUARTER + chunk * width, width)
            lanes = pl.ds(first, width)
            total = acc[:, lanes] + jnp.dot(
                grad, tok[start : start + count, lanes], preferred_element_type=jnp.float32
            )
            total = total * (1.0 / D**0.5)
            for r in range(ZH):
                piece = jnp.concatenate(
                    [
                        total[r * THIRD : (r + 1) * THIRD, s * lanes_of : (s + 1) * lanes_of]
                        for s in range(subs)
                    ],
                    axis=0,
                ).astype(jnp.bfloat16)
                if slots is None:
                    psend[chunk, q * ZH + r] = piece
                elif j == 0:
                    precv[chunk, q * ZH + turned(r)] = piece
                else:
                    psend[chunk, q * ZH + turned(r)] = piece
            if slots is None:
                for i in range(ZH - 1 if j == 0 else ZH):
                    p_copy(chunk, q * ZH + (third + 1 + i) % ZH).start()
            elif j > 0 and chunk == 0:
                x_copy(0, chunk, q, x, 1).start()
        if slots is not None and chunk == 0:
            x_start(0, chunk, 0)

    for chunk in range(chunks):
        last_products(chunk)
    if slots is not None:
        for others in (1, 0):
            x_start(0, 1, others)

    def combine(coefficients, values):
        total = coefficients[0] * values[0]
        for c, v in zip(coefficients[1:], values[1:]):
            total = total + c * v
        return total

    def row_tiles(work):
        @pl.loop(0, part_rows // 16)
        def _(i):
            work(pl.ds(pl.multiple_of(i * 16, 16), 16))

    def f32(value):
        return value.astype(jnp.float32)

    def own_copy(chunk):
        if slots is None:
            return pltpu.make_async_copy(asend.at[chunk, path], arecv.at[chunk, path], own_sem.at[chunk])
        return pltpu.make_async_copy(asend.at[chunk, of_x(x)], arecv.at[chunk, of_x(x)], own_sem.at[chunk])

    def own_average(chunk):
        for o in range(1, NP):
            p_arrival(chunk, (path + o) % NP).wait_recv()
        mine_ = pltpu.make_async_copy(psend.at[chunk, path], precv.at[chunk, path], own_sem.at[chunk])
        mine_.start()
        mine_.wait()

        def work(part):
            values = [f32(precv[chunk, h, part]) for h in range(NP)]
            for g in range(NP):
                total = combine([share[g * NP + h] for h in range(NP)], values)
                asend[chunk, g, part] = (total * inv[g]).astype(jnp.bfloat16)

        row_tiles(work)
        own_copy(chunk).start()
        for o in range(1, NP):
            a_copy(chunk, (path + o) % NP).start()

    def partial_sums(chunk):
        x_wait(0, chunk, 1)
        if chunk + 2 < chunks:
            for others in (1, 0):
                x_start(0, chunk + 2, others)

        def work(part):
            for i in range(ZH - 1):
                values = [f32(precv[chunk, g * ZH + 1 + i, part]) for g in range(NX)]
                for j in range(slots):
                    zbuf[0, chunk, i, j, part] = combine(partial_of[j], values).astype(jnp.bfloat16)

        row_tiles(work)
        for o in range(1, ZH):
            z_copy(0, chunk, o).start()

    def totals(chunk):
        for o in range(1, ZH):
            z_copy(0, chunk, o).wait_recv()
        x_wait(0, chunk, 0)

        def work(part):
            values = [f32(precv[chunk, g * ZH, part]) for g in range(NX)]
            values += [f32(zbuf[1, chunk, i, j, part]) for i in range(ZH - 1) for j in range(slots)]
            for i in range(ZH - 1):
                for j in range(slots):
                    zbuf[2, chunk, i, j, part] = combine(totals_of[i][j], values).astype(jnp.bfloat16)
            for g in range(NX):
                asend[chunk, g * ZH, part] = combine(averages_of[g], values).astype(jnp.bfloat16)

        row_tiles(work)
        for o in range(1, ZH):
            z_copy(1, chunk, o).start()
        x_start(1, chunk, 0)

    def spread(chunk):
        for o in range(1, ZH):
            z_copy(1, chunk, o).wait_recv()

        def work(part):
            for i in range(ZH - 1):
                values = [f32(zbuf[3, chunk, i, j, part]) for j in range(slots)]
                values += [f32(precv[chunk, g * ZH + 1 + i, part]) for g in range(NX)]
                for g in range(NX):
                    asend[chunk, g * ZH + 1 + i, part] = combine(spread_of[g], values).astype(jnp.bfloat16)

        row_tiles(work)
        x_start(1, chunk, 1)
        own_copy(chunk).start()

    def write(chunk, q):
        lanes = slice(q * QUARTER + chunk * width, q * QUARTER + (chunk + 1) * width)
        return pltpu.make_async_copy(fresh.at[:, lanes], out.at[:, lanes], out_sem.at[chunk, q])

    def update(chunk):
        own_copy(chunk).wait()
        if slots is None:
            for o in range(1, NP):
                a_arrival(chunk, (path + o) % NP).wait_recv()
        else:
            x_wait(1, chunk, 0)
            x_wait(1, chunk, 1)
        for q in range(NX):
            for s in range(subs):
                first = q * QUARTER + chunk * width + s * lanes_of
                lanes = slice(first, first + lanes_of)
                averaged = jnp.concatenate(
                    [
                        arecv[chunk, q * ZH + (r if slots is None else turned(r))].astype(jnp.float32)[s * THIRD : (s + 1) * THIRD]
                        for r in range(ZH)
                    ],
                    axis=0,
                )
                moment = 0.9 * mom[:, lanes] + averaged
                new = w[:, lanes].astype(jnp.float32) - 0.7 * (averaged + 0.9 * moment)
                fresh[:, lanes] = new.astype(jnp.bfloat16)
            write(chunk, q).start()

    loads[3].wait()
    if slots is None:
        for chunk in range(chunks):
            own_average(chunk)
        for chunk in range(chunks):
            update(chunk)
    else:
        for chunk in range(chunks):
            partial_sums(chunk)
        for step in range(chunks + 2):
            for late, act in ((0, totals), (1, spread), (2, update)):
                if 0 <= step - late < chunks:
                    act(step - late)

    for block in BLOCKS:
        for_hops(*block, lambda copy: copy.wait_send())
    for chunk in range(chunks):
        if slots is None:
            for o in range(1, NP):
                p_copy(chunk, (path + o) % NP).wait_send()
                a_copy(chunk, (path + o) % NP).wait_send()
        else:
            for back in (0, 1):
                for o in range(1, NX):
                    for others in (0, 1):
                        x_copy(back, chunk, (x + o) % NX, x, others).wait_send()
                for o in range(1, ZH):
                    z_copy(back, chunk, o).wait_send()
    for chunk in range(chunks):
        for q in range(NX):
            write(chunk, q).wait()


def outer_step(slots, number, *arrays):
    dma = pltpu.SemaphoreType.DMA
    bf16, f32 = jnp.bfloat16, jnp.float32
    anywhere = pl.BlockSpec(memory_space=pl.ANY)
    scalars = pl.BlockSpec(memory_space=pltpu.SMEM)
    chunks, lanes_of = (2, 256) if slots is None else (4, 128)
    part_rows = THIRD * QUARTER // (chunks * lanes_of)
    shard = pltpu.VMEM((chunks, NP, part_rows, lanes_of), bf16)
    return pl.pallas_call(
        functools.partial(body, slots, chunks, lanes_of),
        out_shape=jax.ShapeDtypeStruct((COLS, D), bf16),
        in_specs=[anywhere] * 5 + [scalars] * 2,
        out_specs=anywhere,
        scratch_shapes=[
            pltpu.VMEM((TOK, D), bf16),
            pltpu.VMEM((COLS, TOK), bf16),
            pltpu.VMEM((COLS, TOK), bf16),
            pltpu.VMEM((COLS, D), bf16),
            pltpu.VMEM((COLS, D), f32),
            pltpu.VMEM((COLS, D), f32),
            shard, shard, shard, shard,
            pltpu.VMEM((4, chunks, ZH - 1, slots or 1, part_rows, lanes_of), bf16),
            pltpu.VMEM((COLS, D), bf16),
            pltpu.SMEM((NP * NP,), f32),
            pltpu.SMEM((NP,), f32),
            pltpu.SMEM((NP,), jnp.int32),
            dma((4,)),
            dma((chunks,)),
            dma((4, NY, ZL)), dma((NY, ZL)),
            dma((NY, ZL)), dma((NY, ZL)),
            dma((chunks, NP)), dma((chunks, NP)),
            dma((chunks, NP)), dma((chunks, NP)),
            dma((2, chunks, ZH - 1)), dma((2, chunks, ZH - 1)),
            dma((chunks, NX)),
        ],
        compiler_params=pltpu.CompilerParams(
            collective_id=number, has_side_effects=True, vmem_limit_bytes=62 * 2**20
        ),
        name="outer_step",
    )(*arrays)


def widest_plane(table, most):
    result = jnp.int32(0)
    for r in range(ZH):
        shared = jnp.int32(0)
        for xx in range(NX):
            name = table[xx * ZH + r]
            counts = functools.reduce(jnp.logical_or, [table[g] == name for g in range(NP) if g % ZH != r])
            for before in range(xx):
                counts = counts & (table[before * ZH + r] != name)
            shared = shared + jnp.where(counts, 1, 0)
        result = jnp.maximum(result, shared)
    most[0] = jnp.maximum(result, 2) - 2


def on_device(tokens, up_values, out_grad, weights, momentum, path_table, live_tokens):
    scalars = pl.BlockSpec(memory_space=pltpu.SMEM)
    table = path_table[:, 0]
    most = pl.pallas_call(
        widest_plane, out_shape=jax.ShapeDtypeStruct((1,), jnp.int32),
        in_specs=[scalars], out_specs=scalars, name="widest_plane",
    )(table)[0]
    arrays = (tokens[0], up_values[0].T, out_grad[0].T, weights[0].T, momentum[0].T, table, live_tokens)
    new = lax.switch(
        most,
        [functools.partial(outer_step, slots, number) for number, slots in enumerate((2, 3, None))],
        *arrays,
    )
    return new.T[None]


def solution(mesh):
    return jax.shard_map(
        on_device,
        mesh=mesh,
        in_specs=(
            P("path", "fsdp", None),
            P("path", None, "fsdp"),
            P("path", None, "fsdp"),
            P("path", None, "fsdp"),
            P("path", None, "fsdp"),
            P(),
            P("path"),
        ),
        out_specs=P("path", None, "fsdp"),
        check_vma=False,
    )
```
